32 devices in a mesh: dp: 4 (over x, core), blk: 8 (over z, y).
Axes of the slice: x: 2, y: 2, z: 4, core: 2. Of those that a mesh axis runs over, the one named last changes fastest.
Arguments:
- query: bfloat16 [256, 768], P(('dp', 'blk')), parts along dimension 0, may hold values from -6 to 6
- keys: bfloat16 [8192, 768], P(('dp', 'blk')), parts along dimension 0, may hold values from -6 to 6
- values: bfloat16 [8192, 768], P(('dp', 'blk')), parts along dimension 0, may hold values from -6 to 6
- attn_out: bfloat16 [256, 768], P(('dp', 'blk')), parts along dimension 0, may hold values from -1.5 to 1.5
- out_grad: bfloat16 [256, 768], P(('dp', 'blk')), parts along dimension 0, may hold values from -3072 to 3072
- lse: float32 [6, 256], P(None, ('dp', 'blk')), parts along dimension 1, may hold values from 8.5 to 11
- lengths: int32 [256], P(('dp', 'blk')), parts along dimension 0, may hold values from 256 to 2048
Outputs:
- query_grad: bfloat16 [256, 768], P(('dp', 'blk')), parts along dimension 0
- key_grad: bfloat16 [8192, 768], P(('dp', 'blk')), parts along dimension 0
- value_grad: bfloat16 [8192, 768], P(('dp', 'blk')), parts along dimension 0
The draws below stay inside these ranges and needn't reach their ends.
There are 4 independent parts, one for each index of `dp`. The reference program is written for one: setup_inputs(seed, part) draws one part's arguments, and reference() takes and returns one part's arrays. A program takes and returns all parts, laid end to end along the dimension named above; each array names one. Nothing has to cross between parts.
All inputs are finite; a program needn't handle non-finite values.
Results may differ from the reference program's by a relative error of at most 0.005.
Values may be sent and summed in bfloat16 or wider, within the bound.
A program may use at most 64 MiB of HBM per device.

```python
import math
import jax
import jax.numpy as jnp

HEADS = 6
HEAD_DIM = 128
HD = 768
S = 2048
NQ = 64


def plant(array, stream_key, smallest, largest):
    index_at = [jax.random.randint(jax.random.fold_in(stream_key, axis), (), 0, length) for axis, length in enumerate(array.shape)]
    longest = array.shape.index(max(array.shape))
    neighbour = index_at[:longest] + [(index_at[longest] + 1) % array.shape[longest]] + index_at[longest + 1:]
    return array.at[tuple(index_at)].set(smallest).at[tuple(neighbour)].set(largest)


def steps_of(stream_key, extent, split, low, top_value):
    def one(position, parts):
        draws = jax.random.uniform(jax.random.fold_in(jax.random.fold_in(stream_key, 6), position), (parts,), jnp.float32, low / len(split), top_value / len(split))
        return jnp.repeat(jnp.exp(draws), extent[position] // parts).reshape((-1,) + (1,) * (len(extent) - position - 1))

    loudness = one(*split[0])
    for cut in split[1:]:
        loudness = loudness * one(*cut)
    return loudness


def scatter_about(key, extent, scale, limit, split=(), kind=jnp.bfloat16):
    drawn = scale * jax.random.normal(key, extent, jnp.float32)
    if split:
        drawn = drawn * steps_of(key, extent, split, -0.22, 0.18)
    return jnp.clip(drawn, -limit, limit).astype(kind)


def setup_inputs(seed: int = 0, part: int = 0) -> dict:
    seeds = jax.random.split(jax.random.key(seed), 8)
    part_keys = jax.random.split(jax.random.fold_in(seeds[7], part), 8)
    query = scatter_about(part_keys[0], (NQ, HD), 1.0, 6.0, ((0, 8),))
    keys = scatter_about(part_keys[1], (S, HD), 1.0, 6.0, ((0, 8),))
    values = scatter_about(part_keys[2], (S, HD), 1.0, 6.0, ((0, 8),))
    attn_out = scatter_about(part_keys[3], (NQ, HD), 0.25, 1.5, ((0, 8),))
    out_grad = scatter_about(part_keys[4], (NQ, HD), 512.0, 3072.0, ((0, 8),))
    lse = jnp.clip(8.5 + 2.5 * jax.random.uniform(part_keys[5], (HEADS, NQ), jnp.float32) ** steps_of(part_keys[5], (HEADS, NQ), ((1, 8),), -0.2, 0.2), 8.5, 11.0)
    lengths = plant(jax.random.randint(part_keys[6], (NQ,), S // 8, S + 1), jax.random.fold_in(part_keys[6], 1), S // 8, S).astype(jnp.int32)
    return {"query": query, "keys": keys, "values": values, "attn_out": attn_out, "out_grad": out_grad, "lse": lse, "lengths": lengths}


def reference(query, keys, values, attn_out, out_grad, lse, lengths):
    scale = 1.0 / math.sqrt(HEAD_DIM)
    product = out_grad.astype(jnp.float32) * attn_out.astype(jnp.float32)
    delta = product.reshape(NQ, HEADS, HEAD_DIM).sum(axis=-1)
    positions = jnp.arange(S, dtype=jnp.int32)
    visible = positions[None, :] < lengths[:, None]
    query_parts, key_parts, value_parts = ([], [], [])
    for head in range(HEADS):
        low = head * HEAD_DIM
        query_h = query[:, low:low + HEAD_DIM]
        keys_h = keys[:, low:low + HEAD_DIM]
        values_h = values[:, low:low + HEAD_DIM]
        grad_h = out_grad[:, low:low + HEAD_DIM]
        scores = jnp.dot(query_h, keys_h.T, preferred_element_type=jnp.float32) * scale
        probs = jnp.where(visible, jnp.exp(scores - lse[head][:, None]), jnp.float32(0.0))
        probs_low = probs.astype(jnp.bfloat16)
        value_parts.append(jnp.dot(probs_low.T, grad_h, preferred_element_type=jnp.float32))
        prob_grad = jnp.dot(grad_h, values_h.T, preferred_element_type=jnp.float32)
        score_grad = (probs * (prob_grad - delta[:, head][:, None]) * scale).astype(jnp.bfloat16)
        key_parts.append(jnp.dot(score_grad.T, query_h, preferred_element_type=jnp.float32))
        query_parts.append(jnp.dot(score_grad, keys_h, preferred_element_type=jnp.float32))
    query_grad = jnp.concatenate(query_parts, axis=1).astype(jnp.bfloat16)
    key_grad = jnp.concatenate(key_parts, axis=1).astype(jnp.bfloat16)
    value_grad = jnp.concatenate(value_parts, axis=1).astype(jnp.bfloat16)
    return (query_grad, key_grad, value_grad)
```

```python
import functools
import math

import jax
import jax.numpy as jnp
from jax import lax
from jax.experimental import pallas as pl
from jax.experimental.pallas import tpu as pltpu
from jax.sharding import PartitionSpec as P

HEADS_PER_GROUP = 2
CHUNK_SLOTS = 8
UNROLL_LIMIT = 16
F32 = jnp.float32
BF16 = jnp.bfloat16


def over(count, body):
    if count <= UNROLL_LIMIT:
        for i in range(count):
            body(i)
    else:
        lax.fori_loop(0, count, lambda i, c: (body(i), c)[1], 0)


def kernel(
    n, heads, width,
    query, keys, values, attn_out, out_grad, lse, lengths,
    dq_out, dk_out, dv_out,
    q_own, o_own, g_own, lse_own, len_own, k_in, v_in,
    msg, aux, msg_recv, aux_recv, q_all, g_all, p_all, s_all,
    part, part_recv, own_part, dq, dk, dv,
    in_sem, out_sem, aux_send, aux_sem, msg_send, msg_sem, part_send, part_sem,
):
    me = lax.axis_index("blk")
    rows = q_own.shape[0]
    key_rows = k_in.shape[0]
    group_width = HEADS_PER_GROUP * width
    groups = heads // HEADS_PER_GROUP
    scale = 1.0 / math.sqrt(width)
    chunk_slots = min(n, CHUNK_SLOTS)
    chunk_rows = chunk_slots * rows

    small = [(query, q_own), (attn_out, o_own), (out_grad, g_own), (lse, lse_own), (lengths, len_own)]
    large = [(keys, k_in), (values, v_in)]
    copies = [pltpu.make_async_copy(a, b, in_sem.at[i]) for i, (a, b) in enumerate(small + large)]
    for copy in copies:
        copy.start()

    barrier = pltpu.get_barrier_semaphore()

    def greet(i):
        pl.semaphore_signal(
            barrier, inc=1, device_id={"blk": lax.rem(me + i + 1, n)}, device_id_type=pl.DeviceIdType.MESH
        )

    over(n - 1, greet)

    for copy in copies[: len(small)]:
        copy.wait()
    q32, g32 = q_own[...].astype(F32), g_own[...].astype(F32)
    own = jnp.concatenate([q32, g32], axis=0).astype(BF16)
    for g in range(groups):
        piece = own[:, g * group_width : (g + 1) * group_width]
        msg[g] = piece
        msg_recv[g, n - 1] = piece
    product = g32 * o_own[...].astype(F32)
    lane = lax.broadcasted_iota(jnp.int32, (rows, 128), 1)
    eye = lax.broadcasted_iota(jnp.int32, (rows, rows), 0) == lax.broadcasted_iota(jnp.int32, (rows, rows), 1)

    def column(row):
        return jnp.sum(jnp.where(eye, jnp.broadcast_to(row, (rows, rows)), 0.0), axis=1, keepdims=True)

    table = jnp.where(lane == 2 * heads, column(len_own[...].astype(F32)), 0.0)
    for h in range(heads):
        delta = jnp.sum(product[:, h * width : (h + 1) * width], axis=1, keepdims=True)
        table = jnp.where(lane == h, column(lse_own[h : h + 1, :]), table)
        table = jnp.where(lane == heads + h, delta, table)
    aux[...] = table
    aux_recv[n - 1] = table

    pl.semaphore_wait(barrier, n - 1)

    def remote(src, dst, send, recv, peer):
        return pltpu.make_async_remote_copy(
            src_ref=src, dst_ref=dst, send_sem=send, recv_sem=recv,
            device_id={"blk": peer}, device_id_type=pl.DeviceIdType.MESH,
        )

    def send_aux(i):
        remote(aux, aux_recv.at[i], aux_send, aux_sem, lax.rem(me + i + 1, n)).start()

    over(n - 1, send_aux)
    for g in range(groups):

        def send_msg(i, g=g):
            remote(
                msg.at[g], msg_recv.at[g, i], msg_send.at[g], msg_sem.at[g], lax.rem(me + i + 1, n)
            ).start()

        over(n - 1, send_msg)

    def all_of(ref, sem):
        whole = ref.at[pl.ds(0, n - 1)]
        pltpu.make_async_copy(whole, whole, sem).wait()

    for copy in copies[len(small) :]:
        copy.wait()
    all_of(aux_recv, aux_sem)

    position = me * key_rows + lax.broadcasted_iota(jnp.int32, (chunk_rows, key_rows), 1)
    position = position.astype(F32)

    for g in range(groups):
        all_of(msg_recv.at[g], msg_sem.at[g])

        def attend(c, g=g):
            slots = pl.ds(c * chunk_slots, chunk_slots)
            lines = pl.ds(c * chunk_rows, chunk_rows)
            got = msg_recv[g, slots].astype(F32)
            q_c = got[:, :rows].reshape(chunk_rows, group_width).astype(BF16)
            g_c = got[:, rows:].reshape(chunk_rows, group_width).astype(BF16)
            q_all[g, lines] = q_c
            g_all[g, lines] = g_c
            facts = aux_recv[slots].reshape(chunk_rows, 128)
            visible = position < facts[:, 2 * heads : 2 * heads + 1]
            parts = []
            for j in range(HEADS_PER_GROUP):
                h = g * HEADS_PER_GROUP + j
                cols = slice(h * width, (h + 1) * width)
                mine = slice(j * width, (j + 1) * width)
                k_h, v_h = k_in[:, cols], v_in[:, cols]
                nt = (((1,), (1,)), ((), ()))
                scores = lax.dot_general(q_c[:, mine], k_h, nt, preferred_element_type=F32) * scale
                probs = jnp.where(visible, jnp.exp(scores - facts[:, h : h + 1]), 0.0)
                prob_grad = lax.dot_general(g_c[:, mine], v_h, nt, preferred_element_type=F32)
                delta = facts[:, heads + h : heads + h + 1]
                score_grad = (probs * (prob_grad - delta) * scale).astype(BF16)
                p_all[h, lines] = probs.astype(BF16)
                s_all[h, lines] = score_grad
                term = jnp.dot(score_grad, k_h, preferred_element_type=F32)
                parts.append(term.reshape(chunk_slots, rows, width))
            terms = jnp.concatenate(parts, axis=1)
            part[g, slots] = terms.astype(BF16)
            return terms

        if n == chunk_slots:
            own_part[g] = attend(0)[n - 1]
        else:

            def step(c, carry):
                own_part[g] = attend(c)[chunk_slots - 1]
                return carry

            lax.fori_loop(0, n // chunk_slots, step, 0)

        def send_part(i, g=g):
            remote(
                part.at[g, i], part_recv.at[g, i], part_send.at[g], part_sem.at[g], lax.rem(me + n - i - 1, n)
            ).start()

        over(n - 1, send_part)

    tn = (((0,), (0,)), ((), ()))
    results = []
    for g in range(groups):
        for j in range(HEADS_PER_GROUP):
            h = g * HEADS_PER_GROUP + j
            cols = slice(h * width, (h + 1) * width)
            mine = slice(j * width, (j + 1) * width)
            dv[:, cols] = lax.dot_general(p_all[h], g_all[g, :, mine], tn, preferred_element_type=F32).astype(BF16)
            dk[:, cols] = lax.dot_general(s_all[h], q_all[g, :, mine], tn, preferred_element_type=F32).astype(BF16)
    for i, (a, b) in enumerate([(dk, dk_out), (dv, dv_out)]):
        copy = pltpu.make_async_copy(a, b, out_sem.at[i])
        copy.start()
        results.append(copy)

    for g in range(groups):
        all_of(part_recv.at[g], part_sem.at[g])

        def add(i, total, g=g):
            return total + part_recv[g, i].astype(F32)

        total = own_part[g]
        if n <= UNROLL_LIMIT:
            for i in range(n - 1):
                total = add(i, total)
        else:
            total = lax.fori_loop(0, n - 1, add, total)
        for j in range(HEADS_PER_GROUP):
            h = g * HEADS_PER_GROUP + j
            dq[:, h * width : (h + 1) * width] = total[j * rows : (j + 1) * rows].astype(BF16)
    copy = pltpu.make_async_copy(dq, dq_out, out_sem.at[2])
    copy.start()
    results.append(copy)

    all_of(aux_recv, aux_send)
    for g in range(groups):
        all_of(msg_recv.at[g], msg_send.at[g])
        all_of(part_recv.at[g], part_send.at[g])
    for copy in results:
        copy.wait()


def local(n, query, keys, values, attn_out, out_grad, lse, lengths):
    heads, rows = lse.shape
    key_rows, columns = keys.shape
    width = columns // heads
    groups = heads // HEADS_PER_GROUP
    group_width = HEADS_PER_GROUP * width
    total = n * rows
    anywhere = pl.BlockSpec(memory_space=pltpu.HBM)
    vmem = pltpu.VMEM
    dma = pltpu.SemaphoreType.DMA
    return pl.pallas_call(
        functools.partial(kernel, n, heads, width),
        out_shape=(
            jax.ShapeDtypeStruct(query.shape, BF16),
            jax.ShapeDtypeStruct(keys.shape, BF16),
            jax.ShapeDtypeStruct(values.shape, BF16),
        ),
        in_specs=[anywhere] * 7,
        out_specs=(anywhere,) * 3,
        scratch_shapes=[
            vmem(query.shape, BF16),
            vmem(query.shape, BF16),
            vmem(query.shape, BF16),
            vmem(lse.shape, F32),
            vmem((1, rows), jnp.int32),
            vmem(keys.shape, BF16),
            vmem(values.shape, BF16),
            vmem((groups, 2 * rows, group_width), BF16),
            vmem((rows, 128), F32),
            vmem((groups, n, 2 * rows, group_width), BF16),
            vmem((n, rows, 128), F32),
            vmem((groups, total, group_width), BF16),
            vmem((groups, total, group_width), BF16),
            vmem((heads, total, key_rows), BF16),
            vmem((heads, total, key_rows), BF16),
            vmem((groups, n, HEADS_PER_GROUP * rows, width), BF16),
            vmem((groups, n, HEADS_PER_GROUP * rows, width), BF16),
            vmem((groups, HEADS_PER_GROUP * rows, width), F32),
            vmem(query.shape, BF16),
            vmem(keys.shape, BF16),
            vmem(values.shape, BF16),
            dma((7,)),
            dma((3,)),
            dma(()),
            dma(()),
            dma((groups,)),
            dma((groups,)),
            dma((groups,)),
            dma((groups,)),
        ],
        compiler_params=pltpu.CompilerParams(
            collective_id=0, has_side_effects=True, vmem_limit_bytes=40 * 1024 * 1024
        ),
        name="cross_attention_backward",
    )(query, keys, values, attn_out, out_grad, lse, lengths.reshape(1, rows))


def solution(mesh):
    in_specs = (
        P(("dp", "blk"), None),
        P(("dp", "blk"), None),
        P(("dp", "blk"), None),
        P(("dp", "blk"), None),
        P(("dp", "blk"), None),
        P(None, ("dp", "blk")),
        P(("dp", "blk")),
    )
    out_specs = (P(("dp", "blk"), None), P(("dp", "blk"), None), P(("dp", "blk"), None))
    body = functools.partial(local, mesh.shape["blk"])
    return jax.shard_map(body, mesh=mesh, in_specs=in_specs, out_specs=out_specs, check_vma=False)
```

```python
import functools
import math

import jax
import jax.numpy as jnp
from jax import lax
from jax.experimental import pallas as pl
from jax.experimental.pallas import tpu as pltpu
from jax.sharding import PartitionSpec as P

HEADS_PER_GROUP = 2
CHUNK_SLOTS = 8
UNROLL_LIMIT = 16
F32 = jnp.float32
BF16 = jnp.bfloat16


def over(count, body):
    if count <= UNROLL_LIMIT:
        for i in range(count):
            body(i)
    else:
        lax.fori_loop(0, count, lambda i, c: (body(i), c)[1], 0)


def kernel(
    n, heads, width,
    query, keys, values, attn_out, out_grad, lse, lengths,
    dq, dk, dv,
    q_own, o_own, g_own, lse_own, len_own, k_in, v_in,
    msg, aux, msg_recv, aux_recv, q_all, g_all, p_all, s_all,
    part, part_recv, own_part,
    in_sem, aux_send, aux_sem, msg_send, msg_sem, part_send, part_sem,
):
    me = lax.axis_index("blk")
    rows = q_own.shape[0]
    key_rows = k_in.shape[0]
    group_width = HEADS_PER_GROUP * width
    groups = heads // HEADS_PER_GROUP
    scale = 1.0 / math.sqrt(width)
    chunk_slots = min(n, CHUNK_SLOTS)
    chunk_rows = chunk_slots * rows

    small = [(query, q_own), (attn_out, o_own), (out_grad, g_own), (lse, lse_own), (lengths, len_own)]
    large = [(keys, k_in), (values, v_in)]
    copies = [pltpu.make_async_copy(a, b, in_sem.at[i]) for i, (a, b) in enumerate(small + large)]
    for copy in copies:
        copy.start()

    barrier = pltpu.get_barrier_semaphore()

    def greet(i):
        pl.semaphore_signal(
            barrier, inc=1, device_id={"blk": lax.rem(me + i + 1, n)}, device_id_type=pl.DeviceIdType.MESH
        )

    over(n - 1, greet)

    for copy in copies[: len(small)]:
        copy.wait()
    q32, g32 = q_own[...].astype(F32), g_own[...].astype(F32)
    own = jnp.concatenate([q32, g32], axis=0).astype(BF16)
    for g in range(groups):
        piece = own[:, g * group_width : (g + 1) * group_width]
        msg[g] = piece
        msg_recv[g, n - 1] = piece
    product = g32 * o_own[...].astype(F32)
    lane = lax.broadcasted_iota(jnp.int32, (rows, 128), 1)
    eye = lax.broadcasted_iota(jnp.int32, (rows, rows), 0) == lax.broadcasted_iota(jnp.int32, (rows, rows), 1)

    def column(row):
        return jnp.sum(jnp.where(eye, jnp.broadcast_to(row, (rows, rows)), 0.0), axis=1, keepdims=True)

    table = jnp.where(lane == 2 * heads, column(len_own[...].astype(F32)), 0.0)
    for h in range(heads):
        delta = jnp.sum(product[:, h * width : (h + 1) * width], axis=1, keepdims=True)
        table = jnp.where(lane == h, column(lse_own[h : h + 1, :]), table)
        table = jnp.where(lane == heads + h, delta, table)
    aux[...] = table
    aux_recv[n - 1] = table

    pl.semaphore_wait(barrier, n - 1)

    def remote(src, dst, send, recv, peer):
        return pltpu.make_async_remote_copy(
            src_ref=src, dst_ref=dst, send_sem=send, recv_sem=recv,
            device_id={"blk": peer}, device_id_type=pl.DeviceIdType.MESH,
        )

    def send_aux(i):
        remote(aux, aux_recv.at[i], aux_send, aux_sem, lax.rem(me + i + 1, n)).start()

    over(n - 1, send_aux)
    for g in range(groups):

        def send_msg(i, g=g):
            remote(
                msg.at[g], msg_recv.at[g, i], msg_send.at[g], msg_sem.at[g], lax.rem(me + i + 1, n)
            ).start()

        over(n - 1, send_msg)

    def all_of(ref, sem):
        whole = ref.at[pl.ds(0, n - 1)]
        pltpu.make_async_copy(whole, whole, sem).wait()

    for copy in copies[len(small) :]:
        copy.wait()
    all_of(aux_recv, aux_sem)

    position = me * key_rows + lax.broadcasted_iota(jnp.int32, (chunk_rows, key_rows), 1)
    position = position.astype(F32)

    for g in range(groups):
        all_of(msg_recv.at[g], msg_sem.at[g])

        def attend(c, g=g):
            slots = pl.ds(c * chunk_slots, chunk_slots)
            lines = pl.ds(c * chunk_rows, chunk_rows)
            got = msg_recv[g, slots].astype(F32)
            q_c = got[:, :rows].reshape(chunk_rows, group_width).astype(BF16)
            g_c = got[:, rows:].reshape(chunk_rows, group_width).astype(BF16)
            q_all[g, lines] = q_c
            g_all[g, lines] = g_c
            facts = aux_recv[slots].reshape(chunk_rows, 128)
            visible = position < facts[:, 2 * heads : 2 * heads + 1]
            parts = []
            for j in range(HEADS_PER_GROUP):
                h = g * HEADS_PER_GROUP + j
                cols = slice(h * width, (h + 1) * width)
                mine = slice(j * width, (j + 1) * width)
                k_h, v_h = k_in[:, cols], v_in[:, cols]
                nt = (((1,), (1,)), ((), ()))
                scores = lax.dot_general(q_c[:, mine], k_h, nt, preferred_element_type=F32) * scale
                probs = jnp.where(visible, jnp.exp(scores - facts[:, h : h + 1]), 0.0)
                prob_grad = lax.dot_general(g_c[:, mine], v_h, nt, preferred_element_type=F32)
                delta = facts[:, heads + h : heads + h + 1]
                score_grad = (probs * (prob_grad - delta) * scale).astype(BF16)
                p_all[h, lines] = probs.astype(BF16)
                s_all[h, lines] = score_grad
                term = jnp.dot(score_grad, k_h, preferred_element_type=F32)
                parts.append(term.reshape(chunk_slots, rows, width))
            terms = jnp.concatenate(parts, axis=1)
            part[g, slots] = terms.astype(BF16)
            return terms

        if n == chunk_slots:
            own_part[g] = attend(0)[n - 1]
        else:

            def step(c, carry):
                own_part[g] = attend(c)[chunk_slots - 1]
                return carry

            lax.fori_loop(0, n // chunk_slots, step, 0)

        def send_part(i, g=g):
            remote(
                part.at[g, i], part_recv.at[g, i], part_send.at[g], part_sem.at[g], lax.rem(me + n - i - 1, n)
            ).start()

        over(n - 1, send_part)

    tn = (((0,), (0,)), ((), ()))
    for g in range(groups):
        for j in range(HEADS_PER_GROUP):
            h = g * HEADS_PER_GROUP + j
            cols = slice(h * width, (h + 1) * width)
            mine = slice(j * width, (j + 1) * width)
            dv[:, cols] = lax.dot_general(p_all[h], g_all[g, :, mine], tn, preferred_element_type=F32).astype(BF16)
            dk[:, cols] = lax.dot_general(s_all[h], q_all[g, :, mine], tn, preferred_element_type=F32).astype(BF16)

    for g in range(groups):
        all_of(part_recv.at[g], part_sem.at[g])

        def add(i, total, g=g):
            return total + part_recv[g, i].astype(F32)

        total = own_part[g]
        if n <= UNROLL_LIMIT:
            for i in range(n - 1):
                total = add(i, total)
        else:
            total = lax.fori_loop(0, n - 1, add, total)
        for j in range(HEADS_PER_GROUP):
            h = g * HEADS_PER_GROUP + j
            dq[:, h * width : (h + 1) * width] = total[j * rows : (j + 1) * rows].astype(BF16)

    all_of(aux_recv, aux_send)
    for g in range(groups):
        all_of(msg_recv.at[g], msg_send.at[g])
        all_of(part_recv.at[g], part_send.at[g])


def store(dq, dk, dv, dq_out, dk_out, dv_out, sem):
    copies = [
        pltpu.make_async_copy(a, b, sem.at[i])
        for i, (a, b) in enumerate([(dk, dk_out), (dv, dv_out), (dq, dq_out)])
    ]
    for copy in copies:
        copy.start()
    for copy in copies:
        copy.wait()


def local(n, query, keys, values, attn_out, out_grad, lse, lengths):
    heads, rows = lse.shape
    key_rows, columns = keys.shape
    width = columns // heads
    groups = heads // HEADS_PER_GROUP
    group_width = HEADS_PER_GROUP * width
    total = n * rows
    anywhere = pl.BlockSpec(memory_space=pl.ANY)
    vmem = pltpu.VMEM
    dma = pltpu.SemaphoreType.DMA
    arrays = (query, keys, values, attn_out, out_grad, lse, lengths.reshape(1, rows))
    grads = pl.pallas_call(
        functools.partial(kernel, n, heads, width),
        out_shape=(
            jax.ShapeDtypeStruct(query.shape, BF16),
            jax.ShapeDtypeStruct(keys.shape, BF16),
            jax.ShapeDtypeStruct(values.shape, BF16),
        ),
        in_specs=[anywhere] * 7,
        out_specs=(pl.BlockSpec(memory_space=vmem),) * 3,
        scratch_shapes=[
            vmem(query.shape, BF16),
            vmem(query.shape, BF16),
            vmem(query.shape, BF16),
            vmem(lse.shape, F32),
            vmem((1, rows), jnp.int32),
            vmem(keys.shape, BF16),
            vmem(values.shape, BF16),
            vmem((groups, 2 * rows, group_width), BF16),
            vmem((rows, 128), F32),
            vmem((groups, n, 2 * rows, group_width), BF16),
            vmem((n, rows, 128), F32),
            vmem((groups, total, group_width), BF16),
            vmem((groups, total, group_width), BF16),
            vmem((heads, total, key_rows), BF16),
            vmem((heads, total, key_rows), BF16),
            vmem((groups, n, HEADS_PER_GROUP * rows, width), BF16),
            vmem((groups, n, HEADS_PER_GROUP * rows, width), BF16),
            vmem((groups, HEADS_PER_GROUP * rows, width), F32),
            dma((7,)),
            dma(()),
            dma(()),
            dma((groups,)),
            dma((groups,)),
            dma((groups,)),
            dma((groups,)),
        ],
        compiler_params=pltpu.CompilerParams(
            collective_id=0, has_side_effects=True, vmem_limit_bytes=40 * 1024 * 1024
        ),
        name="cross_attention_backward",
    )(*[pltpu.with_memory_space_constraint(a, pltpu.HBM) for a in arrays])
    return pl.pallas_call(
        store,
        out_shape=tuple(jax.ShapeDtypeStruct(a.shape, a.dtype) for a in grads),
        in_specs=[pl.BlockSpec(memory_space=vmem)] * 3,
        out_specs=(anywhere,) * 3,
        scratch_shapes=[dma((3,))],
        compiler_params=pltpu.CompilerParams(vmem_limit_bytes=4 * 1024 * 1024),
        name="store_gradients",
    )(*grads)


def solution(mesh):
    in_specs = (
        P(("dp", "blk"), None),
        P(("dp", "blk"), None),
        P(("dp", "blk"), None),
        P(("dp", "blk"), None),
        P(("dp", "blk"), None),
        P(None, ("dp", "blk")),
        P(("dp", "blk")),
    )
    out_specs = (P(("dp", "blk"), None), P(("dp", "blk"), None), P(("dp", "blk"), None))
    body = functools.partial(local, mesh.shape["blk"])
    return jax.shard_map(body, mesh=mesh, in_specs=in_specs, out_specs=out_specs, check_vma=False)
```

```python
import functools
import math

import jax
import jax.numpy as jnp
from jax import lax
from jax.experimental import pallas as pl
from jax.experimental.pallas import tpu as pltpu
from jax.sharding import PartitionSpec as P

HEADS_PER_GROUP = 2
CHUNK_SLOTS = 8
SEND_ORDER = (0, 1)
UNROLL_LIMIT = 16
F32 = jnp.float32
BF16 = jnp.bfloat16


def over(low, high, body):
    if high - low <= UNROLL_LIMIT:
        for i in reversed(range(low, high)):
            body(i)
    else:
        lax.fori_loop(low, high, lambda i, c: (body(high - 1 + low - i), c)[1], 0)


def kernel(
    n, heads, width,
    query, keys, values, attn_out, out_grad, lse, lengths,
    dq, dk, dv,
    q_own, o_own, g_own, lse_own, len_own, k_in, v_in,
    msg, aux, msg_recv, aux_recv, q_all, g_all, p_all, s_all,
    part, part_recv, own_part,
    in_sem, aux_send, aux_sem, msg_send, msg_sem, part_send, part_sem,
):
    me = lax.axis_index("blk")
    rows = q_own.shape[0]
    key_rows = k_in.shape[0]
    group_width = HEADS_PER_GROUP * width
    groups = heads // HEADS_PER_GROUP
    scale = 1.0 / math.sqrt(width)
    chunk_slots = min(n // 2, CHUNK_SLOTS)
    chunk_rows = chunk_slots * rows
    classes = [(0, n // 2), (n // 2, n)]

    barrier = pltpu.get_barrier_semaphore()

    def greet(i):
        pl.semaphore_signal(
            barrier, inc=1, device_id={"blk": jnp.bitwise_xor(me, i)}, device_id_type=pl.DeviceIdType.MESH
        )

    over(1, n, greet)

    small = [(query, q_own), (attn_out, o_own), (out_grad, g_own), (lse, lse_own), (lengths, len_own)]
    large = [(keys, k_in), (values, v_in)]
    copies = [pltpu.make_async_copy(a, b, in_sem.at[i]) for i, (a, b) in enumerate(small + large)]
    for copy in copies:
        copy.start()

    for copy in copies[: len(small)]:
        copy.wait()
    q32, g32 = q_own[...].astype(F32), g_own[...].astype(F32)
    own = jnp.concatenate([q32, g32], axis=0).astype(BF16)
    for g in range(groups):
        piece = own[:, g * group_width : (g + 1) * group_width]
        msg[g] = piece
        msg_recv[g, 0] = piece
    product = g32 * o_own[...].astype(F32)
    lane = lax.broadcasted_iota(jnp.int32, (rows, 128), 1)
    eye = lax.broadcasted_iota(jnp.int32, (rows, rows), 0) == lax.broadcasted_iota(jnp.int32, (rows, rows), 1)

    def column(row):
        return jnp.sum(jnp.where(eye, jnp.broadcast_to(row, (rows, rows)), 0.0), axis=1, keepdims=True)

    table = jnp.where(lane == 2 * heads, column(len_own[...].astype(F32)), 0.0)
    for h in range(heads):
        delta = jnp.sum(product[:, h * width : (h + 1) * width], axis=1, keepdims=True)
        table = jnp.where(lane == h, column(lse_own[h : h + 1, :]), table)
        table = jnp.where(lane == heads + h, delta, table)
    aux[...] = table
    aux_recv[0] = table

    pl.semaphore_wait(barrier, n - 1)

    def remote(src, dst, send, recv, peer):
        return pltpu.make_async_remote_copy(
            src_ref=src, dst_ref=dst, send_sem=send, recv_sem=recv,
            device_id={"blk": peer}, device_id_type=pl.DeviceIdType.MESH,
        )

    def send_aux(i):
        remote(aux, aux_recv.at[i], aux_send, aux_sem, jnp.bitwise_xor(me, i)).start()

    over(1, n, send_aux)
    for t in SEND_ORDER:
        low, high = classes[t]
        for g in range(groups):

            def send_msg(i, g=g, t=t):
                remote(
                    msg.at[g], msg_recv.at[g, i], msg_send.at[g, t], msg_sem.at[g, t], jnp.bitwise_xor(me, i)
                ).start()

            over(max(low, 1), high, send_msg)

    def all_of(ref, sem, low=1, high=n):
        low = max(low, 1)
        whole = ref.at[pl.ds(low, high - low)]
        pltpu.make_async_copy(whole, whole, sem).wait()

    for copy in copies[len(small) :]:
        copy.wait()
    all_of(aux_recv, aux_sem)

    position = me * key_rows + lax.broadcasted_iota(jnp.int32, (chunk_rows, key_rows), 1)
    position = position.astype(F32)

    for t, (low, high) in enumerate(classes):
        for g in range(groups):
            all_of(msg_recv.at[g], msg_sem.at[g, t], low, high)

            def attend(c, g=g):
                slots = pl.ds(c * chunk_slots, chunk_slots)
                lines = pl.ds(c * chunk_rows, chunk_rows)
                got = msg_recv[g, slots].astype(F32)
                q_c = got[:, :rows].reshape(chunk_rows, group_width).astype(BF16)
                g_c = got[:, rows:].reshape(chunk_rows, group_width).astype(BF16)
                q_all[g, lines] = q_c
                g_all[g, lines] = g_c
                facts = aux_recv[slots].reshape(chunk_rows, 128)
                visible = position < facts[:, 2 * heads : 2 * heads + 1]
                parts = []
                for j in range(HEADS_PER_GROUP):
                    h = g * HEADS_PER_GROUP + j
                    cols = slice(h * width, (h + 1) * width)
                    mine = slice(j * width, (j + 1) * width)
                    k_h, v_h = k_in[:, cols], v_in[:, cols]
                    nt = (((1,), (1,)), ((), ()))
                    scores = lax.dot_general(q_c[:, mine], k_h, nt, preferred_element_type=F32) * scale
                    probs = jnp.where(visible, jnp.exp(scores - facts[:, h : h + 1]), 0.0)
                    prob_grad = lax.dot_general(g_c[:, mine], v_h, nt, preferred_element_type=F32)
                    delta = facts[:, heads + h : heads + h + 1]
                    score_grad = (probs * (prob_grad - delta) * scale).astype(BF16)
                    p_all[h, lines] = probs.astype(BF16)
                    s_all[h, lines] = score_grad
                    term = jnp.dot(score_grad, k_h, preferred_element_type=F32)
                    parts.append(term.reshape(chunk_slots, rows, width))
                terms = jnp.concatenate(parts, axis=1)
                part[g, slots] = terms.astype(BF16)
                return terms

            first, last = low // chunk_slots, high // chunk_slots
            if last - first == 1:
                terms = attend(first)
                if t == 0:
                    own_part[g] = terms[0]
            else:
                if t == 0:
                    own_part[g] = attend(0)[0]
                lax.fori_loop(max(first, 1), last, lambda c, carry, attend=attend: (attend(c), carry)[1], 0)

            def send_part(i, g=g, t=t):
                remote(
                    part.at[g, i], part_recv.at[g, i], part_send.at[g, t], part_sem.at[g, t], jnp.bitwise_xor(me, i)
                ).start()

            over(max(low, 1), high, send_part)

    tn = (((0,), (0,)), ((), ()))
    for g in range(groups):
        for j in range(HEADS_PER_GROUP):
            h = g * HEADS_PER_GROUP + j
            cols = slice(h * width, (h + 1) * width)
            mine = slice(j * width, (j + 1) * width)
            dv[:, cols] = lax.dot_general(p_all[h], g_all[g, :, mine], tn, preferred_element_type=F32).astype(BF16)
            dk[:, cols] = lax.dot_general(s_all[h], q_all[g, :, mine], tn, preferred_element_type=F32).astype(BF16)

    for g in range(groups):
        for t, (low, high) in enumerate(classes):
            all_of(part_recv.at[g], part_sem.at[g, t], low, high)

        def add(i, total, g=g):
            return total + part_recv[g, i].astype(F32)

        total = own_part[g]
        if n <= UNROLL_LIMIT:
            for i in range(1, n):
                total = add(i, total)
        else:
            total = lax.fori_loop(1, n, add, total)
        for j in range(HEADS_PER_GROUP):
            h = g * HEADS_PER_GROUP + j
            dq[:, h * width : (h + 1) * width] = total[j * rows : (j + 1) * rows].astype(BF16)

    all_of(aux_recv, aux_send)
    for g in range(groups):
        for t, (low, high) in enumerate(classes):
            all_of(msg_recv.at[g], msg_send.at[g, t], low, high)
            all_of(part_recv.at[g], part_send.at[g, t], low, high)


def store(dq, dk, dv, dq_out, dk_out, dv_out, sem):
    copies = [
        pltpu.make_async_copy(a, b, sem.at[i])
        for i, (a, b) in enumerate([(dk, dk_out), (dv, dv_out), (dq, dq_out)])
    ]
    for copy in copies:
        copy.start()
    for copy in copies:
        copy.wait()


def local(n, query, keys, values, attn_out, out_grad, lse, lengths):
    heads, rows = lse.shape
    key_rows, columns = keys.shape
    width = columns // heads
    groups = heads // HEADS_PER_GROUP
    group_width = HEADS_PER_GROUP * width
    total = n * rows
    anywhere = pl.BlockSpec(memory_space=pl.ANY)
    vmem = pltpu.VMEM
    dma = pltpu.SemaphoreType.DMA
    arrays = (query, keys, values, attn_out, out_grad, lse, lengths.reshape(1, rows))
    grads = pl.pallas_call(
        functools.partial(kernel, n, heads, width),
        out_shape=(
            jax.ShapeDtypeStruct(query.shape, BF16),
            jax.ShapeDtypeStruct(keys.shape, BF16),
            jax.ShapeDtypeStruct(values.shape, BF16),
        ),
        in_specs=[anywhere] * 7,
        out_specs=(pl.BlockSpec(memory_space=vmem),) * 3,
        scratch_shapes=[
            vmem(query.shape, BF16),
            vmem(query.shape, BF16),
            vmem(query.shape, BF16),
            vmem(lse.shape, F32),
            vmem((1, rows), jnp.int32),
            vmem(keys.shape, BF16),
            vmem(values.shape, BF16),
            vmem((groups, 2 * rows, group_width), BF16),
            vmem((rows, 128), F32),
            vmem((groups, n, 2 * rows, group_width), BF16),
            vmem((n, rows, 128), F32),
            vmem((groups, total, group_width), BF16),
            vmem((groups, total, group_width), BF16),
            vmem((heads, total, key_rows), BF16),
            vmem((heads, total, key_rows), BF16),
            vmem((groups, n, HEADS_PER_GROUP * rows, width), BF16),
            vmem((groups, n, HEADS_PER_GROUP * rows, width), BF16),
            vmem((groups, HEADS_PER_GROUP * rows, width), F32),
            dma((7,)),
            dma(()),
            dma(()),
            dma((groups, 2)),
            dma((groups, 2)),
            dma((groups, 2)),
            dma((groups, 2)),
        ],
        compiler_params=pltpu.CompilerParams(
            collective_id=0, has_side_effects=True, vmem_limit_bytes=40 * 1024 * 1024
        ),
        name="cross_attention_backward",
    )(*[pltpu.with_memory_space_constraint(a, pltpu.HBM) for a in arrays])
    return pl.pallas_call(
        store,
        out_shape=tuple(jax.ShapeDtypeStruct(a.shape, a.dtype) for a in grads),
        in_specs=[pl.BlockSpec(memory_space=vmem)] * 3,
        out_specs=(anywhere,) * 3,
        scratch_shapes=[dma((3,))],
        compiler_params=pltpu.CompilerParams(vmem_limit_bytes=4 * 1024 * 1024),
        name="store_gradients",
    )(*grads)


def solution(mesh):
    in_specs = (
        P(("dp", "blk"), None),
        P(("dp", "blk"), None),
        P(("dp", "blk"), None),
        P(("dp", "blk"), None),
        P(("dp", "blk"), None),
        P(None, ("dp", "blk")),
        P(("dp", "blk")),
    )
    out_specs = (P(("dp", "blk"), None), P(("dp", "blk"), None), P(("dp", "blk"), None))
    body = functools.partial(local, mesh.shape["blk"])
    return jax.shard_map(body, mesh=mesh, in_specs=in_specs, out_specs=out_specs, check_vma=False)
```

```python
import functools
import math

import jax
import jax.numpy as jnp
from jax import lax
from jax.experimental import pallas as pl
from jax.experimental.pallas import tpu as pltpu
from jax.sharding import PartitionSpec as P

HEADS_PER_GROUP = 2
CHUNK_SLOTS = 8
SEND_ORDER = (0, 1)
UNROLL_LIMIT = 16
F32 = jnp.float32
BF16 = jnp.bfloat16


def over(low, high, body):
    if high - low <= UNROLL_LIMIT:
        for i in reversed(range(low, high)):
            body(i)
    else:
        lax.fori_loop(low, high, lambda i, c: (body(high - 1 + low - i), c)[1], 0)


def kernel(
    n, heads, width,
    query, keys, values, attn_out, out_grad, lse, lengths,
    dq, dk, dv,
    q_own, o_own, g_own, lse_own, len_own, k_in, v_in,
    msg, aux, msg_recv, aux_recv, q_all, g_all, p_all, s_all, k_turned, v_turned,
    part, part_recv, own_part,
    in_sem, aux_send, aux_sem, msg_send, msg_sem, part_send, part_sem,
):
    me = lax.axis_index("blk")
    rows = q_own.shape[0]
    key_rows = k_in.shape[0]
    group_width = HEADS_PER_GROUP * width
    groups = heads // HEADS_PER_GROUP
    scale = 1.0 / math.sqrt(width)
    chunk_slots = min(n // 2, CHUNK_SLOTS)
    chunk_rows = chunk_slots * rows
    classes = [(0, n // 2), (n // 2, n)]

    barrier = pltpu.get_barrier_semaphore()

    def greet(i):
        pl.semaphore_signal(
            barrier, inc=1, device_id={"blk": jnp.bitwise_xor(me, i)}, device_id_type=pl.DeviceIdType.MESH
        )

    over(1, n, greet)

    small = [(query, q_own), (attn_out, o_own), (out_grad, g_own), (lse, lse_own), (lengths, len_own)]
    large = [(keys, k_in), (values, v_in)]
    copies = [pltpu.make_async_copy(a, b, in_sem.at[i]) for i, (a, b) in enumerate(small + large)]
    for copy in copies:
        copy.start()

    for copy in copies[: len(small)]:
        copy.wait()
    q32, g32 = q_own[...].astype(F32), g_own[...].astype(F32)
    own = jnp.concatenate([q32, g32], axis=0).astype(BF16)
    for g in range(groups):
        piece = own[:, g * group_width : (g + 1) * group_width]
        msg[g] = piece
        msg_recv[g, 0] = piece
    product = g32 * o_own[...].astype(F32)
    lane = lax.broadcasted_iota(jnp.int32, (rows, 128), 1)
    eye = lax.broadcasted_iota(jnp.int32, (rows, rows), 0) == lax.broadcasted_iota(jnp.int32, (rows, rows), 1)

    def column(row):
        return jnp.sum(jnp.where(eye, jnp.broadcast_to(row, (rows, rows)), 0.0), axis=1, keepdims=True)

    table = jnp.where(lane == 2 * heads, column(len_own[...].astype(F32)), 0.0)
    for h in range(heads):
        delta = jnp.sum(product[:, h * width : (h + 1) * width], axis=1, keepdims=True)
        table = jnp.where(lane == h, column(lse_own[h : h + 1, :]), table)
        table = jnp.where(lane == heads + h, delta, table)
    aux[...] = table
    aux_recv[0] = table

    pl.semaphore_wait(barrier, n - 1)

    def remote(src, dst, send, recv, peer):
        return pltpu.make_async_remote_copy(
            src_ref=src, dst_ref=dst, send_sem=send, recv_sem=recv,
            device_id={"blk": peer}, device_id_type=pl.DeviceIdType.MESH,
        )

    def send_aux(i, t):
        remote(aux, aux_recv.at[i], aux_send.at[t], aux_sem.at[t], jnp.bitwise_xor(me, i)).start()

    for t in SEND_ORDER:
        low, high = classes[t]
        over(max(low, 1), high, functools.partial(send_aux, t=t))
        for g in range(groups):

            def send_msg(i, g=g, t=t):
                remote(
                    msg.at[g], msg_recv.at[g, i], msg_send.at[g, t], msg_sem.at[g, t], jnp.bitwise_xor(me, i)
                ).start()

            over(max(low, 1), high, send_msg)

    def all_of(ref, sem, low=1, high=n):
        low = max(low, 1)
        whole = ref.at[pl.ds(low, high - low)]
        pltpu.make_async_copy(whole, whole, sem).wait()

    for copy in copies[len(small) :]:
        copy.wait()

    for h in range(heads):
        cols = slice(h * width, (h + 1) * width)
        k_turned[h] = k_in[:, cols].T
        v_turned[h] = v_in[:, cols].T

    position = me * key_rows + lax.broadcasted_iota(jnp.int32, (chunk_rows, key_rows), 1)
    position = position.astype(F32)

    for t, (low, high) in enumerate(classes):
        all_of(aux_recv, aux_sem.at[t], low, high)
        for g in range(groups):
            all_of(msg_recv.at[g], msg_sem.at[g, t], low, high)

            def attend(c, g=g):
                slots = pl.ds(c * chunk_slots, chunk_slots)
                lines = pl.ds(c * chunk_rows, chunk_rows)
                got = msg_recv[g, slots].astype(F32)
                q_c = got[:, :rows].reshape(chunk_rows, group_width).astype(BF16)
                g_c = got[:, rows:].reshape(chunk_rows, group_width).astype(BF16)
                q_all[g, lines] = q_c
                g_all[g, lines] = g_c
                facts = aux_recv[slots].reshape(chunk_rows, 128)
                visible = position < facts[:, 2 * heads : 2 * heads + 1]
                parts = []
                for j in range(HEADS_PER_GROUP):
                    h = g * HEADS_PER_GROUP + j
                    cols = slice(h * width, (h + 1) * width)
                    mine = slice(j * width, (j + 1) * width)
                    k_h = k_in[:, cols]
                    scores = jnp.dot(q_c[:, mine], k_turned[h], preferred_element_type=F32) * scale
                    probs = jnp.where(visible, jnp.exp(scores - facts[:, h : h + 1]), 0.0)
                    prob_grad = jnp.dot(g_c[:, mine], v_turned[h], preferred_element_type=F32)
                    delta = facts[:, heads + h : heads + h + 1]
                    score_grad = (probs * (prob_grad - delta) * scale).astype(BF16)
                    p_all[h, lines] = probs.astype(BF16)
                    s_all[h, lines] = score_grad
                    term = jnp.dot(score_grad, k_h, preferred_element_type=F32)
                    parts.append(term.reshape(chunk_slots, rows, width))
                terms = jnp.concatenate(parts, axis=1)
                part[g, slots] = terms.astype(BF16)
                return terms

            first, last = low // chunk_slots, high // chunk_slots
            if last - first == 1:
                terms = attend(first)
                if t == 0:
                    own_part[g] = terms[0]
            else:
                if t == 0:
                    own_part[g] = attend(0)[0]
                lax.fori_loop(max(first, 1), last, lambda c, carry, attend=attend: (attend(c), carry)[1], 0)

            def send_part(i, g=g, t=t):
                remote(
                    part.at[g, i], part_recv.at[g, i], part_send.at[g, t], part_sem.at[g, t], jnp.bitwise_xor(me, i)
                ).start()

            over(max(low, 1), high, send_part)

    tn = (((0,), (0,)), ((), ()))
    for g in range(groups):
        for j in range(HEADS_PER_GROUP):
            h = g * HEADS_PER_GROUP + j
            cols = slice(h * width, (h + 1) * width)
            mine = slice(j * width, (j + 1) * width)
            dv[:, cols] = lax.dot_general(p_all[h], g_all[g, :, mine], tn, preferred_element_type=F32).astype(BF16)
            dk[:, cols] = lax.dot_general(s_all[h], q_all[g, :, mine], tn, preferred_element_type=F32).astype(BF16)

    for g in range(groups):
        for t, (low, high) in enumerate(classes):
            all_of(part_recv.at[g], part_sem.at[g, t], low, high)

        def add(i, total, g=g):
            return total + part_recv[g, i].astype(F32)

        total = own_part[g]
        if n <= UNROLL_LIMIT:
            for i in range(1, n):
                total = add(i, total)
        else:
            total = lax.fori_loop(1, n, add, total)
        for j in range(HEADS_PER_GROUP):
            h = g * HEADS_PER_GROUP + j
            dq[:, h * width : (h + 1) * width] = total[j * rows : (j + 1) * rows].astype(BF16)

    for t, (low, high) in enumerate(classes):
        all_of(aux_recv, aux_send.at[t], low, high)
    for g in range(groups):
        for t, (low, high) in enumerate(classes):
            all_of(msg_recv.at[g], msg_send.at[g, t], low, high)
            all_of(part_recv.at[g], part_send.at[g, t], low, high)


def store(dq, dk, dv, dq_out, dk_out, dv_out, sem):
    copies = [
        pltpu.make_async_copy(a, b, sem.at[i])
        for i, (a, b) in enumerate([(dk, dk_out), (dv, dv_out), (dq, dq_out)])
    ]
    for copy in copies:
        copy.start()
    for copy in copies:
        copy.wait()


def local(n, query, keys, values, attn_out, out_grad, lse, lengths):
    heads, rows = lse.shape
    key_rows, columns = keys.shape
    width = columns // heads
    groups = heads // HEADS_PER_GROUP
    group_width = HEADS_PER_GROUP * width
    total = n * rows
    anywhere = pl.BlockSpec(memory_space=pl.ANY)
    vmem = pltpu.VMEM
    dma = pltpu.SemaphoreType.DMA
    arrays = (query, keys, values, attn_out, out_grad, lse, lengths.reshape(1, rows))
    grads = pl.pallas_call(
        functools.partial(kernel, n, heads, width),
        out_shape=(
            jax.ShapeDtypeStruct(query.shape, BF16),
            jax.ShapeDtypeStruct(keys.shape, BF16),
            jax.ShapeDtypeStruct(values.shape, BF16),
        ),
        in_specs=[anywhere] * 7,
        out_specs=(pl.BlockSpec(memory_space=vmem),) * 3,
        scratch_shapes=[
            vmem(query.shape, BF16),
            vmem(query.shape, BF16),
            vmem(query.shape, BF16),
            vmem(lse.shape, F32),
            vmem((1, rows), jnp.int32),
            vmem(keys.shape, BF16),
            vmem(values.shape, BF16),
            vmem((groups, 2 * rows, group_width), BF16),
            vmem((rows, 128), F32),
            vmem((groups, n, 2 * rows, group_width), BF16),
            vmem((n, rows, 128), F32),
            vmem((groups, total, group_width), BF16),
            vmem((groups, total, group_width), BF16),
            vmem((heads, total, key_rows), BF16),
            vmem((heads, total, key_rows), BF16),
            vmem((heads, width, key_rows), BF16),
            vmem((heads, width, key_rows), BF16),
            vmem((groups, n, HEADS_PER_GROUP * rows, width), BF16),
            vmem((groups, n, HEADS_PER_GROUP * rows, width), BF16),
            vmem((groups, HEADS_PER_GROUP * rows, width), F32),
            dma((7,)),
            dma((2,)),
            dma((2,)),
            dma((groups, 2)),
            dma((groups, 2)),
            dma((groups, 2)),
            dma((groups, 2)),
        ],
        compiler_params=pltpu.CompilerParams(
            collective_id=0, has_side_effects=True, vmem_limit_bytes=40 * 1024 * 1024
        ),
        name="cross_attention_backward",
    )(*[pltpu.with_memory_space_constraint(a, pltpu.HBM) for a in arrays])
    return pl.pallas_call(
        store,
        out_shape=tuple(jax.ShapeDtypeStruct(a.shape, a.dtype) for a in grads),
        in_specs=[pl.BlockSpec(memory_space=vmem)] * 3,
        out_specs=(anywhere,) * 3,
        scratch_shapes=[dma((3,))],
        compiler_params=pltpu.CompilerParams(vmem_limit_bytes=4 * 1024 * 1024),
        name="store_gradients",
    )(*grads)


def solution(mesh):
    in_specs = (
        P(("dp", "blk"), None),
        P(("dp", "blk"), None),
        P(("dp", "blk"), None),
        P(("dp", "blk"), None),
        P(("dp", "blk"), None),
        P(None, ("dp", "blk")),
        P(("dp", "blk")),
    )
    out_specs = (P(("dp", "blk"), None), P(("dp", "blk"), None), P(("dp", "blk"), None))
    body = functools.partial(local, mesh.shape["blk"])
    return jax.shard_map(body, mesh=mesh, in_specs=in_specs, out_specs=out_specs, check_vma=False)
```

```python
import functools
import math

import jax
import jax.numpy as jnp
from jax import lax
from jax.experimental import pallas as pl
from jax.experimental.pallas import tpu as pltpu
from jax.sharding import PartitionSpec as P

HEADS_PER_GROUP = 2
CHUNK_SLOTS = 8
SEND_ORDER = (0, 1)
UNROLL_LIMIT = 16
F32 = jnp.float32
BF16 = jnp.bfloat16


def over(low, high, body):
    if high - low <= UNROLL_LIMIT:
        for i in reversed(range(low, high)):
            body(i)
    else:
        lax.fori_loop(low, high, lambda i, c: (body(high - 1 + low - i), c)[1], 0)


def kernel(
    n, heads, width,
    query, keys, values, attn_out, out_grad, lse, lengths,
    dq, dk, dv,
    q_own, o_own, g_own, lse_own, len_own, k_in, v_in,
    msg, aux, msg_recv, aux_recv, q_all, g_all, p_all, s_all, k_turned, v_turned,
    part, part_recv, own_part,
    in_sem, aux_send, aux_sem, msg_send, msg_sem, part_send, part_sem,
):
    me = lax.axis_index("blk")
    rows = q_own.shape[0]
    key_rows = k_in.shape[0]
    group_width = HEADS_PER_GROUP * width
    groups = heads // HEADS_PER_GROUP
    scale = 1.0 / math.sqrt(width)
    chunk_slots = min(n // 2, CHUNK_SLOTS)
    chunk_rows = chunk_slots * rows
    classes = [(0, n // 2), (n // 2, n)]

    barrier = pltpu.get_barrier_semaphore()

    def greet(i):
        pl.semaphore_signal(
            barrier, inc=1, device_id={"blk": jnp.bitwise_xor(me, i)}, device_id_type=pl.DeviceIdType.MESH
        )

    over(1, n, greet)

    small = [(query, q_own), (attn_out, o_own), (out_grad, g_own), (lse, lse_own), (lengths, len_own)]
    large = [(keys, k_in), (values, v_in)]
    copies = [pltpu.make_async_copy(a, b, in_sem.at[i]) for i, (a, b) in enumerate(small + large)]
    for copy in copies:
        copy.start()

    for copy in copies[: len(small)]:
        copy.wait()
    q32, g32 = q_own[...].astype(F32), g_own[...].astype(F32)
    own = jnp.concatenate([q32, g32], axis=0).astype(BF16)
    for g in range(groups):
        piece = own[:, g * group_width : (g + 1) * group_width]
        msg[g] = piece
        msg_recv[g, 0] = piece
    product = g32 * o_own[...].astype(F32)
    lane = lax.broadcasted_iota(jnp.int32, (rows, 128), 1)
    eye = lax.broadcasted_iota(jnp.int32, (rows, rows), 0) == lax.broadcasted_iota(jnp.int32, (rows, rows), 1)

    def column(row):
        return jnp.sum(jnp.where(eye, jnp.broadcast_to(row, (rows, rows)), 0.0), axis=1, keepdims=True)

    table = jnp.where(lane == 2 * heads, column(len_own[...].astype(F32)), 0.0)
    for h in range(heads):
        delta = jnp.sum(product[:, h * width : (h + 1) * width], axis=1, keepdims=True)
        table = jnp.where(lane == h, column(lse_own[h : h + 1, :]), table)
        table = jnp.where(lane == heads + h, delta, table)
    aux[...] = table
    aux_recv[0] = table

    pl.semaphore_wait(barrier, n - 1)

    def remote(src, dst, send, recv, peer):
        return pltpu.make_async_remote_copy(
            src_ref=src, dst_ref=dst, send_sem=send, recv_sem=recv,
            device_id={"blk": peer}, device_id_type=pl.DeviceIdType.MESH,
        )

    def send_aux(i, t):
        remote(aux, aux_recv.at[i], aux_send.at[t], aux_sem.at[t], jnp.bitwise_xor(me, i)).start()

    for t in SEND_ORDER:
        low, high = classes[t]
        over(max(low, 1), high, functools.partial(send_aux, t=t))
        for g in range(groups):

            def send_msg(i, g=g, t=t):
                remote(
                    msg.at[g], msg_recv.at[g, i], msg_send.at[g, t], msg_sem.at[g, t], jnp.bitwise_xor(me, i)
                ).start()

            over(max(low, 1), high, send_msg)

    def all_of(ref, sem, low=1, high=n):
        low = max(low, 1)
        whole = ref.at[pl.ds(low, high - low)]
        pltpu.make_async_copy(whole, whole, sem).wait()

    for copy in copies[len(small) :]:
        copy.wait()

    for g in range(groups):
        cols = slice(g * group_width, (g + 1) * group_width)
        k_turned[g] = k_in[:, cols].T
        v_turned[g] = v_in[:, cols].T

    position = me * key_rows + lax.broadcasted_iota(jnp.int32, (chunk_rows, key_rows), 1)
    position = position.astype(F32)

    for t, (low, high) in enumerate(classes):
        all_of(aux_recv, aux_sem.at[t], low, high)
        for g in range(groups):
            all_of(msg_recv.at[g], msg_sem.at[g, t], low, high)

            def attend(c, g=g):
                slots = pl.ds(c * chunk_slots, chunk_slots)
                lines = pl.ds(c * chunk_rows, chunk_rows)
                got = msg_recv[g, slots].astype(F32)
                q_c = got[:, :rows].reshape(chunk_rows, group_width).astype(BF16)
                g_c = got[:, rows:].reshape(chunk_rows, group_width).astype(BF16)
                q_all[g, lines] = q_c
                g_all[g, lines] = g_c
                facts = aux_recv[slots].reshape(chunk_rows, 128)
                visible = position < facts[:, 2 * heads : 2 * heads + 1]
                parts = []
                group = slice(g * group_width, (g + 1) * group_width)
                heads_in = [g * HEADS_PER_GROUP + j for j in range(HEADS_PER_GROUP)]
                head_of = lax.broadcasted_iota(jnp.int32, (chunk_rows, group_width), 1) // width

                def spread(x):
                    return jnp.concatenate(
                        [jnp.where(head_of == j, x, jnp.zeros_like(x)) for j in range(HEADS_PER_GROUP)], axis=0
                    )

                scores = jnp.dot(spread(q_c), k_turned[g], preferred_element_type=F32) * scale
                prob_grad = jnp.dot(spread(g_c), v_turned[g], preferred_element_type=F32)
                grads = []
                for j, h in enumerate(heads_in):
                    block = slice(j * chunk_rows, (j + 1) * chunk_rows)
                    probs = jnp.where(visible, jnp.exp(scores[block] - facts[:, h : h + 1]), 0.0)
                    delta = facts[:, heads + h : heads + h + 1]
                    score_grad = (probs * (prob_grad[block] - delta) * scale).astype(BF16)
                    p_all[h, lines] = probs.astype(BF16)
                    s_all[h, lines] = score_grad
                    grads.append(score_grad)
                both = jnp.dot(jnp.concatenate(grads, axis=0), k_in[:, group], preferred_element_type=F32)
                for j in range(HEADS_PER_GROUP):
                    term = both[j * chunk_rows : (j + 1) * chunk_rows, j * width : (j + 1) * width]
                    parts.append(term.reshape(chunk_slots, rows, width))
                terms = jnp.concatenate(parts, axis=1)
                part[g, slots] = terms.astype(BF16)
                return terms

            first, last = low // chunk_slots, high // chunk_slots
            if last - first == 1:
                terms = attend(first)
                if t == 0:
                    own_part[g] = terms[0]
            else:
                if t == 0:
                    own_part[g] = attend(0)[0]
                lax.fori_loop(max(first, 1), last, lambda c, carry, attend=attend: (attend(c), carry)[1], 0)

            def send_part(i, g=g, t=t):
                remote(
                    part.at[g, i], part_recv.at[g, i], part_send.at[g, t], part_sem.at[g, t], jnp.bitwise_xor(me, i)
                ).start()

            over(max(low, 1), high, send_part)

    tn = (((0,), (0,)), ((), ()))
    for g in range(groups):
        for j in range(HEADS_PER_GROUP):
            h = g * HEADS_PER_GROUP + j
            cols = slice(h * width, (h + 1) * width)
            mine = slice(j * width, (j + 1) * width)
            dv[:, cols] = lax.dot_general(p_all[h], g_all[g, :, mine], tn, preferred_element_type=F32).astype(BF16)
            dk[:, cols] = lax.dot_general(s_all[h], q_all[g, :, mine], tn, preferred_element_type=F32).astype(BF16)

    for g in range(groups):
        for t, (low, high) in enumerate(classes):
            all_of(part_recv.at[g], part_sem.at[g, t], low, high)

        def add(i, total, g=g):
            return total + part_recv[g, i].astype(F32)

        total = own_part[g]
        if n <= UNROLL_LIMIT:
            for i in range(1, n):
                total = add(i, total)
        else:
            total = lax.fori_loop(1, n, add, total)
        for j in range(HEADS_PER_GROUP):
            h = g * HEADS_PER_GROUP + j
            dq[:, h * width : (h + 1) * width] = total[j * rows : (j + 1) * rows].astype(BF16)

    for t, (low, high) in enumerate(classes):
        all_of(aux_recv, aux_send.at[t], low, high)
    for g in range(groups):
        for t, (low, high) in enumerate(classes):
            all_of(msg_recv.at[g], msg_send.at[g, t], low, high)
            all_of(part_recv.at[g], part_send.at[g, t], low, high)


def store(dq, dk, dv, dq_out, dk_out, dv_out, sem):
    copies = [
        pltpu.make_async_copy(a, b, sem.at[i])
        for i, (a, b) in enumerate([(dk, dk_out), (dv, dv_out), (dq, dq_out)])
    ]
    for copy in copies:
        copy.start()
    for copy in copies:
        copy.wait()


def local(n, query, keys, values, attn_out, out_grad, lse, lengths):
    heads, rows = lse.shape
    key_rows, columns = keys.shape
    width = columns // heads
    groups = heads // HEADS_PER_GROUP
    group_width = HEADS_PER_GROUP * width
    total = n * rows
    anywhere = pl.BlockSpec(memory_space=pl.ANY)
    vmem = pltpu.VMEM
    dma = pltpu.SemaphoreType.DMA
    arrays = (query, keys, values, attn_out, out_grad, lse, lengths.reshape(1, rows))
    grads = pl.pallas_call(
        functools.partial(kernel, n, heads, width),
        out_shape=(
            jax.ShapeDtypeStruct(query.shape, BF16),
            jax.ShapeDtypeStruct(keys.shape, BF16),
            jax.ShapeDtypeStruct(values.shape, BF16),
        ),
        in_specs=[anywhere] * 7,
        out_specs=(pl.BlockSpec(memory_space=vmem),) * 3,
        scratch_shapes=[
            vmem(query.shape, BF16),
            vmem(query.shape, BF16),
            vmem(query.shape, BF16),
            vmem(lse.shape, F32),
            vmem((1, rows), jnp.int32),
            vmem(keys.shape, BF16),
            vmem(values.shape, BF16),
            vmem((groups, 2 * rows, group_width), BF16),
            vmem((rows, 128), F32),
            vmem((groups, n, 2 * rows, group_width), BF16),
            vmem((n, rows, 128), F32),
            vmem((groups, total, group_width), BF16),
            vmem((groups, total, group_width), BF16),
            vmem((heads, total, key_rows), BF16),
            vmem((heads, total, key_rows), BF16),
            vmem((groups, group_width, key_rows), BF16),
            vmem((groups, group_width, key_rows), BF16),
            vmem((groups, n, HEADS_PER_GROUP * rows, width), BF16),
            vmem((groups, n, HEADS_PER_GROUP * rows, width), BF16),
            vmem((groups, HEADS_PER_GROUP * rows, width), F32),
            dma((7,)),
            dma((2,)),
            dma((2,)),
            dma((groups, 2)),
            dma((groups, 2)),
            dma((groups, 2)),
            dma((groups, 2)),
        ],
        compiler_params=pltpu.CompilerParams(
            collective_id=0, has_side_effects=True, vmem_limit_bytes=40 * 1024 * 1024
        ),
        name="cross_attention_backward",
    )(*[pltpu.with_memory_space_constraint(a, pltpu.HBM) for a in arrays])
    return pl.pallas_call(
        store,
        out_shape=tuple(jax.ShapeDtypeStruct(a.shape, a.dtype) for a in grads),
        in_specs=[pl.BlockSpec(memory_space=vmem)] * 3,
        out_specs=(anywhere,) * 3,
        scratch_shapes=[dma((3,))],
        compiler_params=pltpu.CompilerParams(vmem_limit_bytes=4 * 1024 * 1024),
        name="store_gradients",
    )(*grads)


def solution(mesh):
    in_specs = (
        P(("dp", "blk"), None),
        P(("dp", "blk"), None),
        P(("dp", "blk"), None),
        P(("dp", "blk"), None),
        P(("dp", "blk"), None),
        P(None, ("dp", "blk")),
        P(("dp", "blk")),
    )
    out_specs = (P(("dp", "blk"), None), P(("dp", "blk"), None), P(("dp", "blk"), None))
    body = functools.partial(local, mesh.shape["blk"])
    return jax.shard_map(body, mesh=mesh, in_specs=in_specs, out_specs=out_specs, check_vma=False)
```
